256 devices in a mesh: seq: 64 (over y_lo, x, z), tile: 4 (over y_hi, core).
Axes of the slice: x: 4, y: 4 (y_hi: 2, y_lo: 2; y = y_hi * 2 + y_lo), z: 8, core: 2. Of those that a mesh axis runs over, the one named last changes fastest.
Arguments:
- queries: bfloat16 [16384, 512], P('seq', 'tile'), may hold values from -6 to 6
- keys: bfloat16 [16384, 512], P('seq', 'tile'), may hold values from -6 to 6
- values: bfloat16 [16384, 512], P('seq', 'tile'), may hold values from -6 to 6
- attn_out: bfloat16 [16384, 512], P('seq', 'tile'), may hold values from -6 to 6
- log_norm: float32 [8, 16384], P('tile', 'seq'), as said below
- upstream: bfloat16 [16384, 1024], P('seq', 'tile'), may hold values from -6 to 6
- dec_grad: bfloat16 [16384, 1024], P('seq', 'tile'), may hold values from -6 to 6
- w_dec: bfloat16 [1024, 1024], P(None, 'tile'), may hold values from -0.1875 to 0.1875
- w_out: bfloat16 [512, 1024], P('tile'), may hold values from -0.375 to 0.375
- block_order: int32 [64, 64], P('seq'), may hold values from 0 to 63, each once within a row
Outputs:
- grad_queries: bfloat16 [16384, 512], P('seq', 'tile')
- grad_keys: bfloat16 [16384, 512], P('seq', 'tile')
- grad_values: bfloat16 [16384, 512], P('seq', 'tile')
The draws below stay inside these ranges and needn't reach their ends.
Inputs may be any that keep to these rules, and one draw needn't show every extreme that they name: Row k of block_order is a permutation of the 64 token blocks of index k along seq; entry d names the block that the decoder tile of index d along seq holds as its k-th block. Every entry of log_norm lies between ln(16384) - 0.2 and ln(16384) + 1.2.
All inputs are finite; a program needn't handle non-finite values.
Results may differ from the reference program's by a relative error of at most 0.025.
Values may be sent and summed in bfloat16 or wider, within the bound.
No kernel may reach another device: no remote copies, remote signals or barrier semaphores. Data moves between devices by JAX's collectives and lax.ppermute only.
A program may use at most 128 MiB of HBM per device.

```python
import math
import jax
import jax.numpy as jnp
from jax import lax

D = 1024
HEADS = 8
HD = 64
C = 128
TOKENS = 16384
BLOCKS = 64
BLK = 4


def draw_log_norm(key, part):
    key = jax.random.fold_in(key, 7)
    offset = jax.random.uniform(key, (HEADS, TOKENS), jnp.float32, minval=0.2, maxval=0.8)
    return (math.log(TOKENS) + offset).astype(jnp.float32)


def steps_of(key, dims, shards, low, top_value):
    gain = 1.0
    for position, blocks in shards:
        draws = jax.random.uniform(jax.random.fold_in(jax.random.fold_in(key, 6), position), (blocks,), jnp.float32, low / len(shards), top_value / len(shards))
        gain = gain * jnp.repeat(jnp.exp(draws), dims[position] // blocks).reshape((-1,) + (1,) * (len(dims) - 1 - position))
    return gain


def scatter_about(stream_key, extent, spread, bound, pieces=(), held_as=jnp.bfloat16):
    entries = spread * jax.random.normal(stream_key, extent, jnp.float32)
    if pieces:
        entries = entries * steps_of(stream_key, extent, pieces, -0.22, 0.18)
    return jnp.clip(entries, -bound, bound).astype(held_as)


def setup_inputs(seed: int = 0) -> dict:
    key_of = jax.random.split(jax.random.key(seed), 11)
    return {
        "queries": scatter_about(key_of[0], (TOKENS, HEADS * HD), 1.0, 6.0, ((0, 64), (1, 4))),
        "keys": scatter_about(key_of[1], (TOKENS, HEADS * HD), 1.0, 6.0, ((0, 64), (1, 4))),
        "values": scatter_about(key_of[2], (TOKENS, HEADS * HD), 1.0, 6.0, ((0, 64), (1, 4))),
        "attn_out": scatter_about(key_of[3], (TOKENS, HEADS * HD), 1.0, 6.0, ((0, 64), (1, 4))),
        "log_norm": draw_log_norm(jax.random.fold_in(key_of[10], 71), 0),
        "upstream": scatter_about(key_of[5], (TOKENS, D), 1.0, 6.0, ((0, 64), (1, 4))),
        "dec_grad": scatter_about(key_of[6], (TOKENS, 8 * C), 1.0, 6.0, ((0, 64), (1, 4))),
        "w_dec": scatter_about(key_of[7], (D, 8 * C), (8 * C) ** -0.5, 0.1875, ((1, 4),)),
        "w_out": scatter_about(key_of[8], (HEADS * HD, D), (D // 4) ** -0.5, 0.375, ((0, 4),)),
        "block_order": jax.vmap(lambda own: jax.random.permutation(own, BLOCKS))(jax.random.split(key_of[9], BLOCKS)).reshape((BLOCKS, BLOCKS)).astype(jnp.int32),
    }


def head_grads(inputs):
    query_head, key_head, value_head, grad_head, output_head, norm_head = inputs
    score_scale = 1.0 / math.sqrt(HD)
    row_delta = lax.optimization_barrier(jnp.sum(grad_head.astype(jnp.float32) * output_head.astype(jnp.float32), axis=1))
    block_rows = math.gcd(TOKENS, 1024)
    turn_count = TOKENS // block_rows

    def scan_step(carried, block_data):
        running_k, running_v = carried
        query_blk, grad_blk, norm_blk, delta_blk = block_data
        scores = jnp.dot(query_blk, key_head.T, preferred_element_type=jnp.float32) * score_scale
        attn_probs = jnp.exp(scores - norm_blk[:, None])
        probs_half = attn_probs.astype(jnp.bfloat16)
        running_v = running_v + jnp.dot(probs_half.T, grad_blk, preferred_element_type=jnp.float32)
        d_probs = jnp.dot(grad_blk, value_head.T, preferred_element_type=jnp.float32)
        d_scores = (attn_probs * (d_probs - delta_blk[:, None])).astype(jnp.bfloat16)
        grad_query = jnp.dot(d_scores, key_head, preferred_element_type=jnp.float32) * score_scale
        running_k = running_k + jnp.dot(d_scores.T, query_blk, preferred_element_type=jnp.float32)
        return ((running_k, running_v), grad_query.astype(jnp.bfloat16))
    blocks = (query_head.reshape(turn_count, block_rows, HD), grad_head.reshape(turn_count, block_rows, HD), norm_head.reshape(turn_count, block_rows), row_delta.reshape(turn_count, block_rows))
    zero_acc = jnp.zeros((TOKENS, HD), jnp.float32)
    (running_k, running_v), grad_query = lax.scan(scan_step, (zero_acc, zero_acc), blocks)
    return (grad_query.reshape(TOKENS, HD), (running_k * score_scale).astype(jnp.bfloat16), running_v.astype(jnp.bfloat16))

def heads_first(matrix):
    return matrix.reshape(TOKENS, HEADS, HD).transpose(1, 0, 2)

def heads_last(stacked):
    return stacked.transpose(1, 0, 2).reshape(TOKENS, HEADS * HD)

def reference(queries, keys, values, attn_out, log_norm, upstream, dec_grad, w_dec, w_out, block_order):
    skip_dec = jnp.dot(dec_grad, w_dec.T, preferred_element_type=jnp.float32).astype(jnp.bfloat16)
    arranged = skip_dec.reshape(BLOCKS, BLOCKS, BLK, D).transpose(1, 0, 2, 3)
    inverse = jnp.argsort(block_order, axis=1).astype(jnp.int32)
    placed = jnp.take_along_axis(arranged, inverse[:, :, None, None], axis=1).reshape(TOKENS, D)
    total_grad = (upstream.astype(jnp.float32) + placed.astype(jnp.float32)).astype(jnp.bfloat16)
    d_attn = jnp.dot(total_grad, w_out.T, preferred_element_type=jnp.float32).astype(jnp.bfloat16)
    grad_q, grad_k, grad_v = lax.map(head_grads, (heads_first(queries), heads_first(keys), heads_first(values), heads_first(d_attn), heads_first(attn_out), log_norm))
    return (heads_last(grad_q), heads_last(grad_k), heads_last(grad_v))
```

```python
import jax
import jax.numpy as jnp
from jax import lax
from jax.experimental import pallas as pl
from jax.experimental.pallas import tpu as pltpu
from jax.sharding import Mesh
from jax.sharding import PartitionSpec as P

HD = 64
BLK = 4
SIDE = 8
PAIR = 2
RING = (0, 1, 2, 3, 4, -1, -2, -3)
VMEM = 24 << 20
LARGE = 60 << 20
R = ("yl", "x")
C = "z"
S = ("yl", "x", "z")
T = ("yh", "core")

f32 = jnp.float32
bf16 = jnp.bfloat16


def nt(a, b):
    return lax.dot_general(a, b, (((1,), (1,)), ((), ())), preferred_element_type=f32)


def nn(a, b):
    return lax.dot_general(a, b, (((1,), (0,)), ((), ())), preferred_element_type=f32)


def swap_blocks(x):
    rows = x.shape[0]
    out = lax.broadcasted_iota(jnp.int32, (rows, rows), 0)
    src = lax.broadcasted_iota(jnp.int32, (rows, rows), 1)
    pick = ((out >> 2) & 7) * 32 + (out >> 5) * 4 + (out & 3)
    return nn((src == pick).astype(f32).astype(bf16), x).astype(bf16)


def project_kernel(tile_ref, *refs):
    ins, part_ref, u_refs, copied, sems = refs[:7], refs[7], refs[8:12], refs[12:16], refs[16]
    dec_ref, up_ref, w_dec_ref, w_ref = copied
    outs = [dec_ref, up_ref, w_dec_ref] + [w_ref.at[i * 128 : (i + 1) * 128] for i in range(4)]
    copies = [pltpu.make_async_copy(src, dst, sems.at[i]) for i, (src, dst) in enumerate(zip(ins, outs))]
    for copy in copies:
        copy.start()
    copies[0].wait()
    dec = swap_blocks(dec_ref[...])
    for copy in copies[1:]:
        copy.wait()
    w = nn(w_ref[...], w_dec_ref[...]).astype(bf16)
    part = nt(dec, w).astype(bf16)
    columns = pl.ds(pl.multiple_of(tile_ref[0] * 256, 256), 256)
    u = nt(up_ref[...], w_ref[:, columns]).astype(bf16)
    for i in range(4):
        part_ref[tile_ref[0] ^ i] = part[:, i * 128 : (i + 1) * 128]
        u_refs[i][...] = u[:, i * 128 : (i + 1) * 128]


def project(tile, dec, up, w_dec, w_outs):
    out = pl.pallas_call(
        project_kernel,
        in_specs=[pl.BlockSpec(memory_space=pltpu.SMEM)] + [pl.BlockSpec(memory_space=pl.ANY)] * 7,
        out_shape=[jax.ShapeDtypeStruct((4, 256, 128), bf16)]
        + [jax.ShapeDtypeStruct((256, 128), bf16)] * 4,
        scratch_shapes=[
            pltpu.VMEM(dec.shape, bf16),
            pltpu.VMEM(up.shape, bf16),
            pltpu.VMEM(w_dec.shape, bf16),
            pltpu.VMEM((512, 1024), bf16),
            pltpu.SemaphoreType.DMA((7,)),
        ],
        compiler_params=pltpu.CompilerParams(vmem_limit_bytes=LARGE),
        name="project",
    )(tile, dec, up, w_dec, *w_outs)
    return out[0], out[1:]


def pack_kernel(part_ref, q_ref, out_ref, misc_ref, u0_ref, u1_ref, u2_ref, u3_ref, pay_ref):
    u = u0_ref[...].astype(f32)
    for u_ref in (u1_ref, u2_ref, u3_ref):
        u += u_ref[...].astype(f32)
    u = u.astype(bf16)
    total = part_ref[0].astype(f32)
    for t in range(1, 4):
        total += part_ref[t].astype(f32)
    skip = swap_blocks(total.astype(bf16))
    for r in range(SIDE):
        pay_ref[r, 0:256] = q_ref[...]
        pay_ref[r, 256:512] = out_ref[...]
        pay_ref[r, 512:768] = u
        pay_ref[r, 768:1024] = skip
        pay_ref[r, 1024:1040] = misc_ref[...]


def pack(part, q, out, misc, us):
    return pl.pallas_call(
        pack_kernel,
        out_shape=jax.ShapeDtypeStruct((SIDE, 1040, 128), bf16),
        compiler_params=pltpu.CompilerParams(vmem_limit_bytes=VMEM),
        name="pack",
    )(part, q, out, misc, *us)


def head_masks():
    lane = lax.broadcasted_iota(jnp.int32, (1, 128), 1)
    return [(lane < HD).astype(f32).astype(bf16), (lane >= HD).astype(f32).astype(bf16)]


def token_grads(pay_ref, r):
    rows = 256
    misc = pay_ref[r, 1024:1040].astype(f32)
    dest = jnp.concatenate([misc[12:13], misc[13:14]], 1).astype(jnp.int32)
    token = lax.broadcasted_iota(jnp.int32, (rows, rows), 0)
    place = (token == dest).astype(f32).astype(bf16)
    arrived = pay_ref[:, pl.ds(pl.multiple_of(768 + r * 32, 32), 32)].reshape(rows, 128)
    d_out = (nn(place, arrived) + pay_ref[r, 512:768].astype(f32)).astype(bf16)
    prod = d_out.astype(f32) * pay_ref[r, 256:512].astype(f32)
    hi = prod.astype(bf16)
    rest = prod - hi.astype(f32)
    mid = rest.astype(bf16)
    low = (rest - mid.astype(f32)).astype(bf16)
    sub8 = lax.broadcasted_iota(jnp.int32, (8, 128), 0)
    lane8 = lax.broadcasted_iota(jnp.int32, (8, 128), 1)
    head_rows = (sub8 == lane8 // HD).astype(f32).astype(bf16)
    return d_out, nt(head_rows, hi) + nt(head_rows, mid) + nt(head_rows, low)


def attention_kernel(place_ref, pay_ref, *refs):
    kv_refs = refs[:SIDE]
    dq_ref, vk_ref, kt_ref, dv_acc, dk_acc = refs[SIDE:]
    dv_acc[...] = jnp.zeros_like(dv_acc)
    dk_acc[...] = jnp.zeros_like(dk_acc)
    for t in range(SIDE):
        kt_ref[:, t * 256 : (t + 1) * 256] = kv_refs[t][:, 0:128].astype(f32).T.astype(bf16)

    def step_of(step, carry):
        attention_step(step, place_ref, pay_ref, kv_refs, kt_ref, dq_ref, dv_acc, dk_acc)
        return carry

    lax.fori_loop(0, SIDE // PAIR, step_of, 0)
    for t in range(SIDE):
        c = (place_ref[1] - RING[t]) & (SIDE - 1)
        vk_ref[c, 0] = dv_acc[t * 256 : (t + 1) * 256, :].astype(bf16)
        vk_ref[c, 1] = dk_acc[t * 256 : (t + 1) * 256, :].astype(bf16)


def attention_step(step, place_ref, pay_ref, kv_refs, kt_ref, dq_ref, dv_acc, dk_acc):
    masks = head_masks()
    chains = []
    for i in range(PAIR):
        r = step * PAIR + i
        d_out, delta = token_grads(pay_ref, r)
        query = pay_ref[r, 0:256] * bf16(0.125)
        misc = pay_ref[r, 1024:1040].astype(f32)
        parts = misc[0:4] + misc[4:8] + misc[8:12]
        for h in range(2):
            norm = jnp.concatenate([parts[2 * h : 2 * h + 1], parts[2 * h + 1 : 2 * h + 2]], 1)
            chains.append((h, query * masks[h], d_out * masks[h], norm, delta[h : h + 1, :]))
    queries = jnp.concatenate([chain[1] for chain in chains], 0)
    grads = jnp.concatenate([chain[2] for chain in chains], 0)

    def scores_of(t):
        key, value = kv_refs[t][:, 0:128], kv_refs[t][:, 128:256]
        return [(nt(key, query), nt(value, grad)) for _, query, grad, _, _ in chains]

    dq = [jnp.zeros((HD, 256), f32) for _ in chains]
    later = scores_of(0)
    for t in range(SIDE):
        now = later
        if t + 1 < SIDE:
            later = scores_of(t + 1)
        keys = slice(t * 256, (t + 1) * 256)
        probs, d_scores = [], []
        for i, (h, _, _, norm, delta) in enumerate(chains):
            scores, d_probs = now[i]
            p = jnp.exp(scores - norm)
            d_scores.append((p * (d_probs - delta)).astype(bf16))
            probs.append(p.astype(bf16))
            dq[i] += nn(kt_ref[h * HD : (h + 1) * HD, keys], d_scores[i])
        dv_acc[keys, :] += nn(jnp.concatenate(probs, 1), grads)
        dk_acc[keys, :] += nn(jnp.concatenate(d_scores, 1), queries)
    for i in range(PAIR):
        both = jnp.concatenate(dq[2 * i : 2 * i + 2], 0)
        dq_ref[(step * PAIR + i) ^ place_ref[0]] = (both * 0.125).astype(bf16)


def attention(place, pay, ring):
    dq_shape, vk_shape = (SIDE, 128, 256), (SIDE, 2, 256, 128)
    return pl.pallas_call(
        attention_kernel,
        in_specs=[pl.BlockSpec(memory_space=pltpu.SMEM)] + [pl.BlockSpec(memory_space=pltpu.VMEM)] * 9,
        out_shape=[jax.ShapeDtypeStruct(dq_shape, bf16), jax.ShapeDtypeStruct(vk_shape, bf16)],
        scratch_shapes=[
            pltpu.VMEM((128, SIDE * 256), bf16),
            pltpu.VMEM((SIDE * 256, 128), f32),
            pltpu.VMEM((SIDE * 256, 128), f32),
        ],
        compiler_params=pltpu.CompilerParams(vmem_limit_bytes=VMEM),
        cost_estimate=pl.CostEstimate(flops=20 << 30, bytes_accessed=1 << 23, transcendentals=1 << 23),
        name="attention",
    )(place, pay, *ring)


def finish_kernel(vk_ref, *refs):
    dq_refs, (dq_ref, dk_ref, dv_ref) = refs[:SIDE], refs[SIDE:]

    def total(parts):
        out = parts[0].astype(f32)
        for part in parts[1:]:
            out += part.astype(f32)
        return out

    dq_ref[...] = total([ref[...] for ref in dq_refs]).T.astype(bf16)
    dv_ref[...] = total([vk_ref[i, 0] for i in range(SIDE)]).astype(bf16)
    dk_ref[...] = total([vk_ref[i, 1] for i in range(SIDE)]).astype(bf16)


finish_call = pl.pallas_call(
    finish_kernel,
    out_shape=[jax.ShapeDtypeStruct((256, 128), bf16)] * 3,
    compiler_params=pltpu.CompilerParams(vmem_limit_bytes=VMEM),
    name="finish",
)


def body(queries, keys, values, attn_out, log_norm, upstream, dec_grad, w_dec, w_out, block_order):
    rows, width = queries.shape

    def flip(x, axis):
        return lax.ppermute(x, axis, [(0, 1), (1, 0)])

    def shift(x, axis, by):
        size = lax.axis_size(axis)
        return lax.ppermute(x, axis, [(i, (i + by) % size) for i in range(size)])

    tile = lax.axis_index(T).astype(jnp.int32).reshape(1)
    place = jnp.stack([lax.axis_index(R), lax.axis_index(C)]).astype(jnp.int32)

    def over_tile(x):
        other = flip(x, "yh")
        return x, flip(x, "core"), other, flip(other, "core")

    part, us = project(tile, dec_grad, upstream, w_dec, over_tile(w_out))
    us = [us[0]] + [
        lax.ppermute(us[i], T, [(t, t ^ i) for t in range(4)]) for i in range(1, 4)
    ]
    part = lax.all_to_all(part.reshape(4 * SIDE, 32, width), T + (C,), 0, 0, tiled=True)

    hi = lax.reduce_precision(log_norm, 8, 7)
    mid = lax.reduce_precision(log_norm - hi, 8, 7)
    low = log_norm - hi - mid
    dest = block_order.reshape(-1, 1) * BLK + jnp.arange(BLK, dtype=jnp.int32)
    misc = [a.astype(bf16).reshape(-1, 128) for a in (hi, mid, low, dest)]
    misc = jnp.concatenate(misc + [jnp.zeros((2, 128), bf16)], 0)

    pay = pack(part.reshape(4, rows, width), queries, attn_out, misc, us)
    keys, values, pay = lax.optimization_barrier((keys, values, pay))
    ring = [jnp.concatenate([keys, values], 1)]
    for by, count in ((1, 4), (-1, 3)):
        moved = ring[0]
        for _ in range(count):
            moved = shift(moved, C, by)
            ring.append(moved)
    pay = lax.all_to_all(pay, R, 0, 0, tiled=True)
    dq, vk = attention(place, pay, ring)
    vk = lax.all_to_all(vk, C, 0, 0, tiled=True)
    dq = [dq[0]] + [
        lax.ppermute(dq[s], R, [(i, i ^ s) for i in range(SIDE)]) for s in range(1, SIDE)
    ]
    return tuple(finish_call(vk, *dq))


def solution(mesh):
    grid = Mesh(mesh.devices.reshape(2, 4, 8, 2, 2), S + T)
    return jax.shard_map(
        body,
        mesh=grid,
        in_specs=(
            P(S, T), P(S, T), P(S, T), P(S, T), P(T, S),
            P(S, T), P(S, T), P(None, T), P(T, None), P(S, None),
        ),
        out_specs=(P(S, T), P(S, T), P(S, T)),
        check_vma=False,
    )
```

```python
import functools

import jax
import jax.numpy as jnp
from jax import lax
from jax.experimental import pallas as pl
from jax.experimental.pallas import tpu as pltpu
from jax.sharding import Mesh
from jax.sharding import PartitionSpec as P

HD = 64
BLK = 4
SIDE = 8
PAIR = 2
HALF = 4
FAR = (4, 3, -3, 2)
NEAR = (-2, 1, -1, 0)
VMEM = 24 << 20
LARGE = 60 << 20
R = ("yl", "x")
C = "z"
S = ("yl", "x", "z")
T = ("yh", "core")

f32 = jnp.float32
bf16 = jnp.bfloat16


def nt(a, b):
    return lax.dot_general(a, b, (((1,), (1,)), ((), ())), preferred_element_type=f32)


def nn(a, b):
    return lax.dot_general(a, b, (((1,), (0,)), ((), ())), preferred_element_type=f32)


def swap_blocks(x):
    rows = x.shape[0]
    out = lax.broadcasted_iota(jnp.int32, (rows, rows), 0)
    src = lax.broadcasted_iota(jnp.int32, (rows, rows), 1)
    pick = ((out >> 2) & 7) * 32 + (out >> 5) * 4 + (out & 3)
    return nn((src == pick).astype(f32).astype(bf16), x).astype(bf16)


def project_kernel(tile_ref, *refs):
    ins, part_ref, u_refs, copied, sems = refs[:7], refs[7], refs[8:12], refs[12:16], refs[16]
    dec_ref, up_ref, w_dec_ref, w_ref = copied
    outs = [dec_ref, up_ref, w_dec_ref] + [w_ref.at[i * 128 : (i + 1) * 128] for i in range(4)]
    copies = [pltpu.make_async_copy(src, dst, sems.at[i]) for i, (src, dst) in enumerate(zip(ins, outs))]
    for copy in copies:
        copy.start()
    copies[0].wait()
    dec = swap_blocks(dec_ref[...])
    for copy in copies[1:]:
        copy.wait()
    w = nn(w_ref[...], w_dec_ref[...]).astype(bf16)
    part = nt(dec, w).astype(bf16)
    columns = pl.ds(pl.multiple_of(tile_ref[0] * 256, 256), 256)
    u = nt(up_ref[...], w_ref[:, columns]).astype(bf16)
    for i in range(4):
        part_ref[tile_ref[0] ^ i] = part[:, i * 128 : (i + 1) * 128]
        u_refs[i][...] = u[:, i * 128 : (i + 1) * 128]


def project(tile, dec, up, w_dec, w_outs):
    out = pl.pallas_call(
        project_kernel,
        in_specs=[pl.BlockSpec(memory_space=pltpu.SMEM)] + [pl.BlockSpec(memory_space=pl.ANY)] * 7,
        out_shape=[jax.ShapeDtypeStruct((4, 256, 128), bf16)]
        + [jax.ShapeDtypeStruct((256, 128), bf16)] * 4,
        scratch_shapes=[
            pltpu.VMEM(dec.shape, bf16),
            pltpu.VMEM(up.shape, bf16),
            pltpu.VMEM(w_dec.shape, bf16),
            pltpu.VMEM((512, 1024), bf16),
            pltpu.SemaphoreType.DMA((7,)),
        ],
        compiler_params=pltpu.CompilerParams(vmem_limit_bytes=LARGE),
        name="project",
    )(tile, dec, up, w_dec, *w_outs)
    return out[0], out[1:]


def pack_kernel(part_ref, q_ref, out_ref, misc_ref, u0_ref, u1_ref, u2_ref, u3_ref, pay_ref):
    u = u0_ref[...].astype(f32)
    for u_ref in (u1_ref, u2_ref, u3_ref):
        u += u_ref[...].astype(f32)
    u = u.astype(bf16)
    total = part_ref[0].astype(f32)
    for t in range(1, 4):
        total += part_ref[t].astype(f32)
    skip = swap_blocks(total.astype(bf16))
    for r in range(SIDE):
        pay_ref[r, 0:256] = q_ref[...]
        pay_ref[r, 256:512] = out_ref[...]
        pay_ref[r, 512:768] = u
        pay_ref[r, 768:1024] = skip
        pay_ref[r, 1024:1040] = misc_ref[...]


def pack(part, q, out, misc, us):
    return pl.pallas_call(
        pack_kernel,
        out_shape=jax.ShapeDtypeStruct((SIDE, 1040, 128), bf16),
        compiler_params=pltpu.CompilerParams(vmem_limit_bytes=VMEM),
        name="pack",
    )(part, q, out, misc, *us)


def head_masks():
    lane = lax.broadcasted_iota(jnp.int32, (1, 128), 1)
    return [(lane < HD).astype(f32).astype(bf16), (lane >= HD).astype(f32).astype(bf16)]


def token_grads(pay_ref, r):
    rows = 256
    misc = pay_ref[r, 1024:1040].astype(f32)
    dest = jnp.concatenate([misc[12:13], misc[13:14]], 1).astype(jnp.int32)
    token = lax.broadcasted_iota(jnp.int32, (rows, rows), 0)
    place = (token == dest).astype(f32).astype(bf16)
    arrived = pay_ref[:, pl.ds(pl.multiple_of(768 + r * 32, 32), 32)].reshape(rows, 128)
    d_out = (nn(place, arrived) + pay_ref[r, 512:768].astype(f32)).astype(bf16)
    prod = d_out.astype(f32) * pay_ref[r, 256:512].astype(f32)
    hi = prod.astype(bf16)
    rest = prod - hi.astype(f32)
    mid = rest.astype(bf16)
    low = (rest - mid.astype(f32)).astype(bf16)
    sub8 = lax.broadcasted_iota(jnp.int32, (8, 128), 0)
    lane8 = lax.broadcasted_iota(jnp.int32, (8, 128), 1)
    head_rows = (sub8 == lane8 // HD).astype(f32).astype(bf16)
    return d_out, nt(head_rows, hi) + nt(head_rows, mid) + nt(head_rows, low)


def attention_kernel(far, pay_ref, *refs):
    kv_refs, refs = refs[:HALF], refs[HALF:]
    if far:
        shared, vk_refs, (kt_ref, dv_acc, dk_acc) = refs[:3], refs[3 : 3 + HALF], refs[3 + HALF :]
        dq_out = None
    else:
        shared, dq_out, refs = refs[:3], refs[3], refs[4:]
        vk_refs, (kt_ref, dv_acc, dk_acc) = refs[:HALF], refs[HALF:]
    dv_acc[...] = jnp.zeros_like(dv_acc)
    dk_acc[...] = jnp.zeros_like(dk_acc)
    for t in range(HALF):
        kt_ref[:, t * 256 : (t + 1) * 256] = kv_refs[t][:, 0:128].astype(f32).T.astype(bf16)

    def step_of(step, carry):
        attention_step(step, pay_ref, kv_refs, shared, dq_out, kt_ref, dv_acc, dk_acc)
        return carry

    lax.fori_loop(0, SIDE // PAIR, step_of, 0)
    for t in range(HALF):
        vk_refs[t][0] = dv_acc[t * 256 : (t + 1) * 256, :].astype(bf16)
        vk_refs[t][1] = dk_acc[t * 256 : (t + 1) * 256, :].astype(bf16)


def attention_step(step, pay_ref, kv_refs, shared, dq_out, kt_ref, dv_acc, dk_acc):
    d_out_ref, delta_ref, dq_ref = shared
    masks = head_masks()
    chains = []
    for i in range(PAIR):
        r = step * PAIR + i
        if dq_out is None:
            d_out_ref[r], delta_ref[r] = token_grads(pay_ref, r)
        d_out, delta = d_out_ref[r], delta_ref[r]
        query = pay_ref[r, 0:256] * bf16(0.125)
        misc = pay_ref[r, 1024:1040].astype(f32)
        parts = misc[0:4] + misc[4:8] + misc[8:12]
        for h in range(2):
            norm = jnp.concatenate([parts[2 * h : 2 * h + 1], parts[2 * h + 1 : 2 * h + 2]], 1)
            chains.append((h, query * masks[h], d_out * masks[h], norm, delta[h : h + 1, :]))
    queries = jnp.concatenate([chain[1] for chain in chains], 0)
    grads = jnp.concatenate([chain[2] for chain in chains], 0)

    def scores_of(t):
        key, value = kv_refs[t][:, 0:128], kv_refs[t][:, 128:256]
        return [(nt(key, query), nt(value, grad)) for _, query, grad, _, _ in chains]

    dq = [jnp.zeros((HD, 256), f32) for _ in chains]
    later = scores_of(0)
    for t in range(HALF):
        now = later
        if t + 1 < HALF:
            later = scores_of(t + 1)
        keys = slice(t * 256, (t + 1) * 256)
        probs, d_scores = [], []
        for i, (h, _, _, norm, delta) in enumerate(chains):
            scores, d_probs = now[i]
            p = jnp.exp(scores - norm)
            d_scores.append((p * (d_probs - delta)).astype(bf16))
            probs.append(p.astype(bf16))
            dq[i] += nn(kt_ref[h * HD : (h + 1) * HD, keys], d_scores[i])
        dv_acc[keys, :] += nn(jnp.concatenate(probs, 1), grads)
        dk_acc[keys, :] += nn(jnp.concatenate(d_scores, 1), queries)
    for i in range(PAIR):
        r = step * PAIR + i
        both = jnp.concatenate(dq[2 * i : 2 * i + 2], 0)
        if dq_out is None:
            dq_ref[r] = both
        else:
            dq_out[r] = ((dq_ref[r] + both) * 0.125).astype(bf16)


SHARED = [
    jax.ShapeDtypeStruct((SIDE, 256, 128), bf16),
    jax.ShapeDtypeStruct((SIDE, 8, 256), f32),
    jax.ShapeDtypeStruct((SIDE, 128, 256), f32),
]


def attention(pay, kv, shared=None):
    far = shared is None
    outs = SHARED if far else [jax.ShapeDtypeStruct((SIDE, 128, 256), bf16)]
    ins = [pay, *kv] + ([] if far else list(shared))
    out = pl.pallas_call(
        functools.partial(attention_kernel, far),
        out_shape=outs + [jax.ShapeDtypeStruct((2, 256, 128), bf16)] * HALF,
        scratch_shapes=[
            pltpu.VMEM((128, HALF * 256), bf16),
            pltpu.VMEM((HALF * 256, 128), f32),
            pltpu.VMEM((HALF * 256, 128), f32),
        ],
        compiler_params=pltpu.CompilerParams(vmem_limit_bytes=VMEM),
        cost_estimate=pl.CostEstimate(flops=14 << 30, bytes_accessed=1 << 22, transcendentals=1 << 22),
        name="far" if far else "near",
    )(*ins)
    return out[: len(outs)], out[len(outs) :]


def finish_kernel(*refs):
    vk_refs, (dq_parts, dq_ref, dk_ref, dv_ref) = refs[:SIDE], refs[SIDE:]

    def total(parts):
        out = parts[0].astype(f32)
        for part in parts[1:]:
            out += part.astype(f32)
        return out

    dq_ref[...] = total([dq_parts[i] for i in range(SIDE)]).T.astype(bf16)
    dv_ref[...] = total([ref[0] for ref in vk_refs]).astype(bf16)
    dk_ref[...] = total([ref[1] for ref in vk_refs]).astype(bf16)


finish_call = pl.pallas_call(
    finish_kernel,
    out_shape=[jax.ShapeDtypeStruct((256, 128), bf16)] * 3,
    compiler_params=pltpu.CompilerParams(vmem_limit_bytes=VMEM),
    name="finish",
)


def body(queries, keys, values, attn_out, log_norm, upstream, dec_grad, w_dec, w_out, block_order):
    rows, width = queries.shape

    def flip(x, axis):
        return lax.ppermute(x, axis, [(0, 1), (1, 0)])

    def shift(x, axis, by):
        size = lax.axis_size(axis)
        return lax.ppermute(x, axis, [(i, (i + by) % size) for i in range(size)])

    tile = lax.axis_index(T).astype(jnp.int32).reshape(1)

    def over_tile(x):
        other = flip(x, "yh")
        return x, flip(x, "core"), other, flip(other, "core")

    part, us = project(tile, dec_grad, upstream, w_dec, over_tile(w_out))
    us = [us[0]] + [
        lax.ppermute(us[i], T, [(t, t ^ i) for t in range(4)]) for i in range(1, 4)
    ]
    part = lax.all_to_all(part.reshape(4 * SIDE, 32, width), T + (C,), 0, 0, tiled=True)

    hi = lax.reduce_precision(log_norm, 8, 7)
    mid = lax.reduce_precision(log_norm - hi, 8, 7)
    low = log_norm - hi - mid
    dest = block_order.reshape(-1, 1) * BLK + jnp.arange(BLK, dtype=jnp.int32)
    misc = [a.astype(bf16).reshape(-1, 128) for a in (hi, mid, low, dest)]
    misc = jnp.concatenate(misc + [jnp.zeros((2, 128), bf16)], 0)

    pay = pack(part.reshape(4, rows, width), queries, attn_out, misc, us)
    keys, values, pay = lax.optimization_barrier((keys, values, pay))
    ring = {0: jnp.concatenate([keys, values], 1)}
    for by, count in ((1, 4), (-1, 3)):
        for hop in range(1, count + 1):
            ring[by * hop] = shift(ring[by * (hop - 1)], C, by)
    pay = lax.all_to_all(pay, R, 0, 0, tiled=True)
    shared, vk_far = attention(pay, [ring[s] for s in FAR])
    vk_far = [shift(vk, C, -s) for s, vk in zip(FAR, vk_far)]
    (dq,), vk_near = attention(pay, [ring[s] for s in NEAR], shared)
    vk_near = [shift(vk, C, -s) if s else vk for s, vk in zip(NEAR, vk_near)]
    vk_far, dq = lax.optimization_barrier((vk_far, dq))
    dq = lax.all_to_all(dq, R, 0, 0, tiled=True)
    return tuple(finish_call(*vk_far, *vk_near, dq))


def solution(mesh):
    grid = Mesh(mesh.devices.reshape(2, 4, 8, 2, 2), S + T)
    return jax.shard_map(
        body,
        mesh=grid,
        in_specs=(
            P(S, T), P(S, T), P(S, T), P(S, T), P(T, S),
            P(S, T), P(S, T), P(None, T), P(T, None), P(S, None),
        ),
        out_specs=(P(S, T), P(S, T), P(S, T)),
        check_vma=False,
    )
```

```python
import functools

import jax
import jax.numpy as jnp
from jax import lax
from jax.experimental import pallas as pl
from jax.experimental.pallas import tpu as pltpu
from jax.sharding import Mesh
from jax.sharding import PartitionSpec as P

HD = 64
BLK = 4
SIDE = 8
PAIR = 4
FAR = (4, 3, -3)
NEAR = (2, -2, 1, -1, 0)
VMEM = 24 << 20
LARGE = 60 << 20
R = ("yl", "x")
C = "z"
S = ("yl", "x", "z")
T = ("yh", "core")

f32 = jnp.float32
bf16 = jnp.bfloat16


def nt(a, b):
    return lax.dot_general(a, b, (((1,), (1,)), ((), ())), preferred_element_type=f32)


def nn(a, b):
    return lax.dot_general(a, b, (((1,), (0,)), ((), ())), preferred_element_type=f32)


def swap_blocks(x):
    rows = x.shape[0]
    out = lax.broadcasted_iota(jnp.int32, (rows, rows), 0)
    src = lax.broadcasted_iota(jnp.int32, (rows, rows), 1)
    pick = ((out >> 2) & 7) * 32 + (out >> 5) * 4 + (out & 3)
    return nn((src == pick).astype(f32).astype(bf16), x).astype(bf16)


def project_kernel(tile_ref, *refs):
    ins, part_ref, u_refs, copied, sems = refs[:7], refs[7], refs[8:12], refs[12:16], refs[16]
    dec_ref, up_ref, w_dec_ref, w_ref = copied
    outs = [dec_ref, up_ref, w_dec_ref] + [w_ref.at[i * 128 : (i + 1) * 128] for i in range(4)]
    copies = [pltpu.make_async_copy(src, dst, sems.at[i]) for i, (src, dst) in enumerate(zip(ins, outs))]
    for copy in copies:
        copy.start()
    copies[0].wait()
    dec = swap_blocks(dec_ref[...])
    for copy in copies[1:]:
        copy.wait()
    w = nn(w_ref[...], w_dec_ref[...]).astype(bf16)
    part = nt(dec, w).astype(bf16)
    columns = pl.ds(pl.multiple_of(tile_ref[0] * 256, 256), 256)
    u = nt(up_ref[...], w_ref[:, columns]).astype(bf16)
    for i in range(4):
        part_ref[tile_ref[0] ^ i] = part[:, i * 128 : (i + 1) * 128]
        u_refs[i][...] = u[:, i * 128 : (i + 1) * 128]


def project(tile, dec, up, w_dec, w_outs):
    out = pl.pallas_call(
        project_kernel,
        in_specs=[pl.BlockSpec(memory_space=pltpu.SMEM)] + [pl.BlockSpec(memory_space=pl.ANY)] * 7,
        out_shape=[jax.ShapeDtypeStruct((4, 256, 128), bf16)]
        + [jax.ShapeDtypeStruct((256, 128), bf16)] * 4,
        scratch_shapes=[
            pltpu.VMEM(dec.shape, bf16),
            pltpu.VMEM(up.shape, bf16),
            pltpu.VMEM(w_dec.shape, bf16),
            pltpu.VMEM((512, 1024), bf16),
            pltpu.SemaphoreType.DMA((7,)),
        ],
        compiler_params=pltpu.CompilerParams(vmem_limit_bytes=LARGE),
        name="project",
    )(tile, dec, up, w_dec, *w_outs)
    return out[0], out[1:]


def pack_kernel(part_ref, q_ref, out_ref, misc_ref, u0_ref, u1_ref, u2_ref, u3_ref, pay_ref):
    u = u0_ref[...].astype(f32)
    for u_ref in (u1_ref, u2_ref, u3_ref):
        u += u_ref[...].astype(f32)
    u = u.astype(bf16)
    total = part_ref[0].astype(f32)
    for t in range(1, 4):
        total += part_ref[t].astype(f32)
    skip = swap_blocks(total.astype(bf16))
    for r in range(SIDE):
        pay_ref[r, 0:256] = q_ref[...]
        pay_ref[r, 256:512] = out_ref[...]
        pay_ref[r, 512:768] = u
        pay_ref[r, 768:1024] = skip
        pay_ref[r, 1024:1040] = misc_ref[...]


def pack(part, q, out, misc, us):
    return pl.pallas_call(
        pack_kernel,
        out_shape=jax.ShapeDtypeStruct((SIDE, 1040, 128), bf16),
        compiler_params=pltpu.CompilerParams(vmem_limit_bytes=VMEM),
        name="pack",
    )(part, q, out, misc, *us)


def head_masks():
    lane = lax.broadcasted_iota(jnp.int32, (1, 128), 1)
    return [(lane < HD).astype(f32).astype(bf16), (lane >= HD).astype(f32).astype(bf16)]


def token_grads(pay_ref, r):
    rows = 256
    misc = pay_ref[r, 1024:1040].astype(f32)
    dest = jnp.concatenate([misc[12:13], misc[13:14]], 1).astype(jnp.int32)
    token = lax.broadcasted_iota(jnp.int32, (rows, rows), 0)
    place = (token == dest).astype(f32).astype(bf16)
    arrived = pay_ref[:, pl.ds(pl.multiple_of(768 + r * 32, 32), 32)].reshape(rows, 128)
    d_out = (nn(place, arrived) + pay_ref[r, 512:768].astype(f32)).astype(bf16)
    prod = d_out.astype(f32) * pay_ref[r, 256:512].astype(f32)
    hi = prod.astype(bf16)
    rest = prod - hi.astype(f32)
    mid = rest.astype(bf16)
    low = (rest - mid.astype(f32)).astype(bf16)
    sub8 = lax.broadcasted_iota(jnp.int32, (8, 128), 0)
    lane8 = lax.broadcasted_iota(jnp.int32, (8, 128), 1)
    head_rows = (sub8 == lane8 // HD).astype(f32).astype(bf16)
    return d_out, nt(head_rows, hi) + nt(head_rows, mid) + nt(head_rows, low)


def attention_kernel(far, pay_ref, *refs):
    count = len(FAR if far else NEAR)
    kv_refs, refs = refs[:count], refs[count:]
    if far:
        shared, vk_refs, (kt_ref, dv_acc, dk_acc) = refs[:3], refs[3 : 3 + count], refs[3 + count :]
        dq_out = None
    else:
        shared, dq_out, refs = refs[:3], refs[3], refs[4:]
        vk_refs, (kt_ref, dv_acc, dk_acc) = refs[:count], refs[count:]
    dv_acc[...] = jnp.zeros_like(dv_acc)
    dk_acc[...] = jnp.zeros_like(dk_acc)
    for t in range(count):
        kt_ref[:, t * 256 : (t + 1) * 256] = kv_refs[t][:, 0:128].astype(f32).T.astype(bf16)

    def step_of(step, carry):
        attention_step(step, pay_ref, kv_refs, shared, dq_out, kt_ref, dv_acc, dk_acc)
        return carry

    lax.fori_loop(0, SIDE // PAIR, step_of, 0)
    for t in range(count):
        vk_refs[t][0] = dv_acc[t * 256 : (t + 1) * 256, :].astype(bf16)
        vk_refs[t][1] = dk_acc[t * 256 : (t + 1) * 256, :].astype(bf16)


def attention_step(step, pay_ref, kv_refs, shared, dq_out, kt_ref, dv_acc, dk_acc):
    d_out_ref, delta_ref, dq_ref = shared
    masks = head_masks()
    chains = []
    for i in range(PAIR):
        r = step * PAIR + i
        if dq_out is None:
            d_out_ref[r], delta_ref[r] = token_grads(pay_ref, r)
        d_out, delta = d_out_ref[r], delta_ref[r]
        query = pay_ref[r, 0:256] * bf16(0.125)
        misc = pay_ref[r, 1024:1040].astype(f32)
        parts = misc[0:4] + misc[4:8] + misc[8:12]
        for h in range(2):
            norm = jnp.concatenate([parts[2 * h : 2 * h + 1], parts[2 * h + 1 : 2 * h + 2]], 1)
            chains.append((h, query * masks[h], d_out * masks[h], norm, delta[h : h + 1, :]))
    queries = jnp.concatenate([chain[1] for chain in chains], 0)
    grads = jnp.concatenate([chain[2] for chain in chains], 0)

    def scores_of(t):
        key, value = kv_refs[t][:, 0:128], kv_refs[t][:, 128:256]
        return [(nt(key, query), nt(value, grad)) for _, query, grad, _, _ in chains]

    dq = [jnp.zeros((HD, 256), f32) for _ in chains]
    later = scores_of(0)
    for t in range(len(kv_refs)):
        now = later
        if t + 1 < len(kv_refs):
            later = scores_of(t + 1)
        keys = slice(t * 256, (t + 1) * 256)
        probs, d_scores = [], []
        for i, (h, _, _, norm, delta) in enumerate(chains):
            scores, d_probs = now[i]
            p = jnp.exp(scores - norm)
            d_scores.append((p * (d_probs - delta)).astype(bf16))
            probs.append(p.astype(bf16))
            dq[i] += nn(kt_ref[h * HD : (h + 1) * HD, keys], d_scores[i])
        dv_acc[keys, :] += nn(jnp.concatenate(probs, 1), grads)
        dk_acc[keys, :] += nn(jnp.concatenate(d_scores, 1), queries)
    for i in range(PAIR):
        r = step * PAIR + i
        both = jnp.concatenate(dq[2 * i : 2 * i + 2], 0)
        if dq_out is None:
            dq_ref[r] = both
        else:
            dq_out[r] = ((dq_ref[r] + both) * 0.125).astype(bf16)


SHARED = [
    jax.ShapeDtypeStruct((SIDE, 256, 128), bf16),
    jax.ShapeDtypeStruct((SIDE, 8, 256), f32),
    jax.ShapeDtypeStruct((SIDE, 128, 256), f32),
]


def attention(pay, kv, shared=None):
    far = shared is None
    outs = SHARED if far else [jax.ShapeDtypeStruct((SIDE, 128, 256), bf16)]
    ins = [pay, *kv] + ([] if far else list(shared))
    out = pl.pallas_call(
        functools.partial(attention_kernel, far),
        out_shape=outs + [jax.ShapeDtypeStruct((2, 256, 128), bf16)] * len(kv),
        scratch_shapes=[
            pltpu.VMEM((128, len(kv) * 256), bf16),
            pltpu.VMEM((len(kv) * 256, 128), f32),
            pltpu.VMEM((len(kv) * 256, 128), f32),
        ],
        compiler_params=pltpu.CompilerParams(vmem_limit_bytes=VMEM),
        cost_estimate=pl.CostEstimate(flops=14 << 30, bytes_accessed=1 << 22, transcendentals=1 << 22),
        name="far" if far else "near",
    )(*ins)
    return out[: len(outs)], out[len(outs) :]


def finish_kernel(*refs):
    vk_refs, (dq_parts, dq_ref, dk_ref, dv_ref) = refs[:SIDE], refs[SIDE:]

    def total(parts):
        out = parts[0].astype(f32)
        for part in parts[1:]:
            out += part.astype(f32)
        return out

    dq_ref[...] = total([dq_parts[i] for i in range(SIDE)]).T.astype(bf16)
    dv_ref[...] = total([ref[0] for ref in vk_refs]).astype(bf16)
    dk_ref[...] = total([ref[1] for ref in vk_refs]).astype(bf16)


finish_call = pl.pallas_call(
    finish_kernel,
    out_shape=[jax.ShapeDtypeStruct((256, 128), bf16)] * 3,
    compiler_params=pltpu.CompilerParams(vmem_limit_bytes=VMEM),
    name="finish",
)


def body(queries, keys, values, attn_out, log_norm, upstream, dec_grad, w_dec, w_out, block_order):
    rows, width = queries.shape

    def flip(x, axis):
        return lax.ppermute(x, axis, [(0, 1), (1, 0)])

    def shift(x, axis, by):
        size = lax.axis_size(axis)
        return lax.ppermute(x, axis, [(i, (i + by) % size) for i in range(size)])

    tile = lax.axis_index(T).astype(jnp.int32).reshape(1)

    def over_tile(x):
        other = flip(x, "yh")
        return x, flip(x, "core"), other, flip(other, "core")

    part, us = project(tile, dec_grad, upstream, w_dec, over_tile(w_out))
    us = [us[0]] + [
        lax.ppermute(us[i], T, [(t, t ^ i) for t in range(4)]) for i in range(1, 4)
    ]
    part = lax.all_to_all(part.reshape(4 * SIDE, 32, width), T + (C,), 0, 0, tiled=True)

    hi = lax.reduce_precision(log_norm, 8, 7)
    mid = lax.reduce_precision(log_norm - hi, 8, 7)
    low = log_norm - hi - mid
    dest = block_order.reshape(-1, 1) * BLK + jnp.arange(BLK, dtype=jnp.int32)
    misc = [a.astype(bf16).reshape(-1, 128) for a in (hi, mid, low, dest)]
    misc = jnp.concatenate(misc + [jnp.zeros((2, 128), bf16)], 0)

    pay = pack(part.reshape(4, rows, width), queries, attn_out, misc, us)
    keys, values, pay = lax.optimization_barrier((keys, values, pay))
    ring = {0: jnp.concatenate([keys, values], 1)}
    for by, count in ((1, 4), (-1, 3)):
        for hop in range(1, count + 1):
            ring[by * hop] = shift(ring[by * (hop - 1)], C, by)
    pay = lax.all_to_all(pay, R, 0, 0, tiled=True)
    shared, vk_far = attention(pay, [ring[s] for s in FAR])
    vk_far = [shift(vk, C, -s) for s, vk in zip(FAR, vk_far)]
    (dq,), vk_near = attention(pay, [ring[s] for s in NEAR], shared)
    vk_near = [shift(vk, C, -s) if s else vk for s, vk in zip(NEAR, vk_near)]
    vk_far, dq = lax.optimization_barrier((vk_far, dq))
    dq = lax.all_to_all(dq, R, 0, 0, tiled=True)
    return tuple(finish_call(*vk_far, *vk_near, dq))


def solution(mesh):
    grid = Mesh(mesh.devices.reshape(2, 4, 8, 2, 2), S + T)
    return jax.shard_map(
        body,
        mesh=grid,
        in_specs=(
            P(S, T), P(S, T), P(S, T), P(S, T), P(T, S),
            P(S, T), P(S, T), P(None, T), P(T, None), P(S, None),
        ),
        out_specs=(P(S, T), P(S, T), P(S, T)),
        check_vma=False,
    )
```

```python
import functools

import jax
import jax.numpy as jnp
from jax import lax
from jax.experimental import pallas as pl
from jax.experimental.pallas import tpu as pltpu
from jax.sharding import Mesh
from jax.sharding import PartitionSpec as P

HD = 64
BLK = 4
SIDE = 8
PAIR = 8
FAR = (4, 3, -3)
NEAR = (2, -2, 1, -1, 0)
VMEM = 24 << 20
LARGE = 60 << 20
R = ("yl", "x")
C = "z"
S = ("yl", "x", "z")
T = ("yh", "core")

f32 = jnp.float32
bf16 = jnp.bfloat16


def nt(a, b):
    return lax.dot_general(a, b, (((1,), (1,)), ((), ())), preferred_element_type=f32)


def nn(a, b):
    return lax.dot_general(a, b, (((1,), (0,)), ((), ())), preferred_element_type=f32)


def swap_blocks(x):
    rows = x.shape[0]
    out = lax.broadcasted_iota(jnp.int32, (rows, rows), 0)
    src = lax.broadcasted_iota(jnp.int32, (rows, rows), 1)
    pick = ((out >> 2) & 7) * 32 + (out >> 5) * 4 + (out & 3)
    return nn((src == pick).astype(f32).astype(bf16), x).astype(bf16)


def project_kernel(tile_ref, *refs):
    ins, part_ref, u_refs, copied, sems = refs[:7], refs[7], refs[8:12], refs[12:16], refs[16]
    dec_ref, up_ref, w_dec_ref, w_ref = copied
    outs = [dec_ref, up_ref, w_dec_ref] + [w_ref.at[i * 128 : (i + 1) * 128] for i in range(4)]
    copies = [pltpu.make_async_copy(src, dst, sems.at[i]) for i, (src, dst) in enumerate(zip(ins, outs))]
    for copy in copies:
        copy.start()
    copies[0].wait()
    dec = swap_blocks(dec_ref[...])
    for copy in copies[1:]:
        copy.wait()
    w = nn(w_ref[...], w_dec_ref[...]).astype(bf16)
    part = nt(dec, w).astype(bf16)
    columns = pl.ds(pl.multiple_of(tile_ref[0] * 256, 256), 256)
    u = nt(up_ref[...], w_ref[:, columns]).astype(bf16)
    for i in range(4):
        part_ref[tile_ref[0] ^ i] = part[:, i * 128 : (i + 1) * 128]
        u_refs[i][...] = u[:, i * 128 : (i + 1) * 128]


def project(tile, dec, up, w_dec, w_outs):
    out = pl.pallas_call(
        project_kernel,
        in_specs=[pl.BlockSpec(memory_space=pltpu.SMEM)] + [pl.BlockSpec(memory_space=pl.ANY)] * 7,
        out_shape=[jax.ShapeDtypeStruct((4, 256, 128), bf16)]
        + [jax.ShapeDtypeStruct((256, 128), bf16)] * 4,
        scratch_shapes=[
            pltpu.VMEM(dec.shape, bf16),
            pltpu.VMEM(up.shape, bf16),
            pltpu.VMEM(w_dec.shape, bf16),
            pltpu.VMEM((512, 1024), bf16),
            pltpu.SemaphoreType.DMA((7,)),
        ],
        compiler_params=pltpu.CompilerParams(vmem_limit_bytes=LARGE),
        name="project",
    )(tile, dec, up, w_dec, *w_outs)
    return out[0], out[1:]


def pack_kernel(part_ref, q_ref, out_ref, misc_ref, u0_ref, u1_ref, u2_ref, u3_ref, pay_ref):
    u = u0_ref[...].astype(f32)
    for u_ref in (u1_ref, u2_ref, u3_ref):
        u += u_ref[...].astype(f32)
    u = u.astype(bf16)
    total = part_ref[0].astype(f32)
    for t in range(1, 4):
        total += part_ref[t].astype(f32)
    skip = swap_blocks(total.astype(bf16))
    for r in range(SIDE):
        pay_ref[r, 0:256] = q_ref[...]
        pay_ref[r, 256:512] = out_ref[...]
        pay_ref[r, 512:768] = u
        pay_ref[r, 768:1024] = skip
        pay_ref[r, 1024:1040] = misc_ref[...]


def pack(part, q, out, misc, us):
    return pl.pallas_call(
        pack_kernel,
        out_shape=jax.ShapeDtypeStruct((SIDE, 1040, 128), bf16),
        compiler_params=pltpu.CompilerParams(vmem_limit_bytes=VMEM),
        name="pack",
    )(part, q, out, misc, *us)


def head_masks():
    lane = lax.broadcasted_iota(jnp.int32, (1, 128), 1)
    return [(lane < HD).astype(f32).astype(bf16), (lane >= HD).astype(f32).astype(bf16)]


def token_grads(pay_ref, r):
    rows = 256
    misc = pay_ref[r, 1024:1040].astype(f32)
    dest = jnp.concatenate([misc[12:13], misc[13:14]], 1).astype(jnp.int32)
    token = lax.broadcasted_iota(jnp.int32, (rows, rows), 0)
    place = (token == dest).astype(f32).astype(bf16)
    arrived = pay_ref[:, pl.ds(pl.multiple_of(768 + r * 32, 32), 32)].reshape(rows, 128)
    d_out = (nn(place, arrived) + pay_ref[r, 512:768].astype(f32)).astype(bf16)
    prod = d_out.astype(f32) * pay_ref[r, 256:512].astype(f32)
    hi = prod.astype(bf16)
    rest = prod - hi.astype(f32)
    mid = rest.astype(bf16)
    low = (rest - mid.astype(f32)).astype(bf16)
    sub8 = lax.broadcasted_iota(jnp.int32, (8, 128), 0)
    lane8 = lax.broadcasted_iota(jnp.int32, (8, 128), 1)
    head_rows = (sub8 == lane8 // HD).astype(f32).astype(bf16)
    return d_out, nt(head_rows, hi) + nt(head_rows, mid) + nt(head_rows, low)


def attention_kernel(far, pay_ref, *refs):
    count = len(FAR if far else NEAR)
    kv_refs, refs = refs[:count], refs[count:]
    if far:
        shared, vk_refs, (kt_ref, dv_acc, dk_acc) = refs[:3], refs[3 : 3 + count], refs[3 + count :]
        dq_out = None
    else:
        shared, dq_out, refs = refs[:3], refs[3], refs[4:]
        vk_refs, (kt_ref, dv_acc, dk_acc) = refs[:count], refs[count:]
    dv_acc[...] = jnp.zeros_like(dv_acc)
    dk_acc[...] = jnp.zeros_like(dk_acc)
    for t in range(count):
        kt_ref[:, t * 256 : (t + 1) * 256] = kv_refs[t][:, 0:128].astype(f32).T.astype(bf16)

    def step_of(step, carry):
        attention_step(step, pay_ref, kv_refs, shared, dq_out, kt_ref, dv_acc, dk_acc)
        return carry

    lax.fori_loop(0, SIDE // PAIR, step_of, 0)
    for t in range(count):
        vk_refs[t][0] = dv_acc[t * 256 : (t + 1) * 256, :].astype(bf16)
        vk_refs[t][1] = dk_acc[t * 256 : (t + 1) * 256, :].astype(bf16)


def attention_step(step, pay_ref, kv_refs, shared, dq_out, kt_ref, dv_acc, dk_acc):
    d_out_ref, delta_ref, dq_ref = shared
    masks = head_masks()
    chains = []
    for i in range(PAIR):
        r = step * PAIR + i
        if dq_out is None:
            d_out_ref[r], delta_ref[r] = token_grads(pay_ref, r)
        d_out, delta = d_out_ref[r], delta_ref[r]
        query = pay_ref[r, 0:256] * bf16(0.125)
        misc = pay_ref[r, 1024:1040].astype(f32)
        parts = misc[0:4] + misc[4:8] + misc[8:12]
        for h in range(2):
            norm = jnp.concatenate([parts[2 * h : 2 * h + 1], parts[2 * h + 1 : 2 * h + 2]], 1)
            chains.append((h, query * masks[h], d_out * masks[h], norm, delta[h : h + 1, :]))
    queries = jnp.concatenate([chain[1] for chain in chains], 0)
    grads = jnp.concatenate([chain[2] for chain in chains], 0)

    def scores_of(t):
        key, value = kv_refs[t][:, 0:128], kv_refs[t][:, 128:256]
        return [(nt(key, query), nt(value, grad)) for _, query, grad, _, _ in chains]

    dq = [jnp.zeros((HD, 256), f32) for _ in chains]
    later = scores_of(0)
    for t in range(len(kv_refs)):
        now = later
        if t + 1 < len(kv_refs):
            later = scores_of(t + 1)
        keys = slice(t * 256, (t + 1) * 256)
        probs, d_scores = [], []
        for i, (h, _, _, norm, delta) in enumerate(chains):
            scores, d_probs = now[i]
            p = jnp.exp(scores - norm)
            d_scores.append((p * (d_probs - delta)).astype(bf16))
            probs.append(p.astype(bf16))
            dq[i] += nn(kt_ref[h * HD : (h + 1) * HD, keys], d_scores[i])
        dv_acc[keys, :] += nn(jnp.concatenate(probs, 1), grads)
        dk_acc[keys, :] += nn(jnp.concatenate(d_scores, 1), queries)
    for i in range(PAIR):
        r = step * PAIR + i
        both = jnp.concatenate(dq[2 * i : 2 * i + 2], 0)
        if dq_out is None:
            dq_ref[r] = both
        else:
            dq_out[r] = ((dq_ref[r] + both) * 0.125).astype(bf16)


SHARED = [
    jax.ShapeDtypeStruct((SIDE, 256, 128), bf16),
    jax.ShapeDtypeStruct((SIDE, 8, 256), f32),
    jax.ShapeDtypeStruct((SIDE, 128, 256), f32),
]


def attention(pay, kv, shared=None):
    far = shared is None
    outs = SHARED if far else [jax.ShapeDtypeStruct((SIDE, 128, 256), bf16)]
    ins = [pay, *kv] + ([] if far else list(shared))
    out = pl.pallas_call(
        functools.partial(attention_kernel, far),
        out_shape=outs + [jax.ShapeDtypeStruct((2, 256, 128), bf16)] * len(kv),
        scratch_shapes=[
            pltpu.VMEM((128, len(kv) * 256), bf16),
            pltpu.VMEM((len(kv) * 256, 128), f32),
            pltpu.VMEM((len(kv) * 256, 128), f32),
        ],
        compiler_params=pltpu.CompilerParams(vmem_limit_bytes=44 << 20),
        cost_estimate=pl.CostEstimate(flops=14 << 30, bytes_accessed=1 << 22, transcendentals=1 << 22),
        name="far" if far else "near",
    )(*ins)
    return out[: len(outs)], out[len(outs) :]


def finish_kernel(*refs):
    vk_refs, (dq_parts, dq_ref, dk_ref, dv_ref) = refs[:SIDE], refs[SIDE:]

    def total(parts):
        out = parts[0].astype(f32)
        for part in parts[1:]:
            out += part.astype(f32)
        return out

    dq_ref[...] = total([dq_parts[i] for i in range(SIDE)]).T.astype(bf16)
    dv_ref[...] = total([ref[0] for ref in vk_refs]).astype(bf16)
    dk_ref[...] = total([ref[1] for ref in vk_refs]).astype(bf16)


finish_call = pl.pallas_call(
    finish_kernel,
    out_shape=[jax.ShapeDtypeStruct((256, 128), bf16)] * 3,
    compiler_params=pltpu.CompilerParams(vmem_limit_bytes=VMEM),
    name="finish",
)


def body(queries, keys, values, attn_out, log_norm, upstream, dec_grad, w_dec, w_out, block_order):
    rows, width = queries.shape

    def flip(x, axis):
        return lax.ppermute(x, axis, [(0, 1), (1, 0)])

    def shift(x, axis, by):
        size = lax.axis_size(axis)
        return lax.ppermute(x, axis, [(i, (i + by) % size) for i in range(size)])

    tile = lax.axis_index(T).astype(jnp.int32).reshape(1)

    def over_tile(x):
        other = flip(x, "yh")
        return x, flip(x, "core"), other, flip(other, "core")

    part, us = project(tile, dec_grad, upstream, w_dec, over_tile(w_out))
    us = [us[0]] + [
        lax.ppermute(us[i], T, [(t, t ^ i) for t in range(4)]) for i in range(1, 4)
    ]
    part = lax.all_to_all(part.reshape(4 * SIDE, 32, width), T + (C,), 0, 0, tiled=True)

    hi = lax.reduce_precision(log_norm, 8, 7)
    mid = lax.reduce_precision(log_norm - hi, 8, 7)
    low = log_norm - hi - mid
    dest = block_order.reshape(-1, 1) * BLK + jnp.arange(BLK, dtype=jnp.int32)
    misc = [a.astype(bf16).reshape(-1, 128) for a in (hi, mid, low, dest)]
    misc = jnp.concatenate(misc + [jnp.zeros((2, 128), bf16)], 0)

    pay = pack(part.reshape(4, rows, width), queries, attn_out, misc, us)
    keys, values, pay = lax.optimization_barrier((keys, values, pay))
    ring = {0: jnp.concatenate([keys, values], 1)}
    for by, count in ((1, 4), (-1, 3)):
        for hop in range(1, count + 1):
            ring[by * hop] = shift(ring[by * (hop - 1)], C, by)
    pay = lax.all_to_all(pay, R, 0, 0, tiled=True)
    shared, vk_far = attention(pay, [ring[s] for s in FAR])
    vk_far = [shift(vk, C, -s) for s, vk in zip(FAR, vk_far)]
    (dq,), vk_near = attention(pay, [ring[s] for s in NEAR], shared)
    vk_near = [shift(vk, C, -s) if s else vk for s, vk in zip(NEAR, vk_near)]
    vk_far, dq = lax.optimization_barrier((vk_far, dq))
    dq = lax.all_to_all(dq, R, 0, 0, tiled=True)
    return tuple(finish_call(*vk_far, *vk_near, dq))


def solution(mesh):
    grid = Mesh(mesh.devices.reshape(2, 4, 8, 2, 2), S + T)
    return jax.shard_map(
        body,
        mesh=grid,
        in_specs=(
            P(S, T), P(S, T), P(S, T), P(S, T), P(T, S),
            P(S, T), P(S, T), P(None, T), P(T, None), P(S, None),
        ),
        out_specs=(P(S, T), P(S, T), P(S, T)),
        check_vma=False,
    )
```
